128 devices in a mesh: px: 16 (over z, x), py: 8 (over y, core).
Axes of the slice: x: 4, y: 4, z: 4, core: 2. Of those that a mesh axis runs over, the one named last changes fastest.
Arguments:
- a_tiles: bfloat16 [16384, 19, 64, 64], P(('px', 'py')), may hold values from -0.15625 to 0.15625
- a_cols: int32 [16384, 19], P(('px', 'py')), may hold values from 0 to 16383, as said below
- p_tiles: bfloat16 [16384, 64, 64], P(('px', 'py')), may hold values from -0.75 to 0.75
- aggregate: int32 [16384], P(('px', 'py')), may hold values from 0 to 2047, as said below
Outputs:
- ap_rows: bfloat16 [16384, 64, 64], P(('px', 'py'))
- coarse: float32 [2048, 64, 64], P(('px', 'py'))
The draws below stay inside these ranges and needn't reach their ends.
Inputs may be any that keep to these rules, and one draw needn't show every extreme that they name: `a_cols`: block row g's columns lie in the rows of g's partition or of a partition beside it along px or py (partition of row g is g // 128, numbered px-major, no wrap); column 0 is g itself. `aggregate`: aggregate a is owned by partition a // 16. The 128 rows of one partition fall in aggregates of at most 2 rows for each owner, and some owner gets exactly 2 rows from every partition.
All inputs are finite; a program needn't handle non-finite values.
Results may differ from the reference program's by a relative error of at most 0.0029.
Values may be sent and summed in bfloat16 or wider, within the bound.
No kernel may reach another device: no remote copies, remote signals or barrier semaphores. Data moves between devices by JAX's collectives and lax.ppermute only.
A program may use at most 192 MiB of HBM per device.

```python
import jax
import jax.numpy as jnp
from jax import lax

B = 64
K = 19
ROW_DEV = 128
AGG_DEV = 16
GRID_X = 16
GRID_Y = 8
NDEV = 128
ROWS = 16384
NAGG = 2048
SLOT = 2


def draw_a_cols(key, part):
    key = jax.random.fold_in(key, 1)
    first, second = jax.random.split(key)
    glob = jnp.arange(ROWS, dtype=jnp.int32)
    device = glob // ROW_DEV
    row_x = device // GRID_Y
    row_y = device % GRID_Y
    direction = jax.random.randint(first, (ROWS, K), 0, 5)
    valid = jnp.stack([jnp.ones_like(row_x) > 0, row_x > 0, row_x < GRID_X - 1, row_y > 0, row_y < GRID_Y - 1], axis=1)
    picked = jnp.take_along_axis(valid, direction, axis=1)
    direction = jnp.where(picked, direction, 0)
    offsets = jnp.array([0, -GRID_Y, GRID_Y, -1, 1], dtype=jnp.int32)
    local = jax.random.randint(second, (ROWS, K), 0, ROW_DEV)
    cols = (device[:, None] + offsets[direction]) * ROW_DEV + local
    cols = cols.at[:, 0].set(glob)
    return cols.astype(jnp.int32)


def draw_aggregate(key, part):
    key = jax.random.fold_in(key, 2)
    hot_key, base = jax.random.split(key)
    hot = jax.random.randint(hot_key, (), 0, NDEV)
    entries = jnp.arange(NDEV * SLOT, dtype=jnp.int32)
    owners = entries // SLOT

    def per_device(device):
        dkey = jax.random.fold_in(base, device)
        kone, ktwo, kthree = jax.random.split(dkey, 3)
        perm = jax.random.permutation(kone, NDEV * SLOT).astype(jnp.int32)
        score = jnp.where(owners == hot, -1 - entries % SLOT, perm)
        order = jnp.argsort(score, stable=True)
        chosen = owners[order[:ROW_DEV]]
        chosen = chosen[jax.random.permutation(ktwo, ROW_DEV)]
        local = jax.random.randint(kthree, (ROW_DEV,), 0, AGG_DEV)
        return chosen * AGG_DEV + local
    result = jax.vmap(per_device)(jnp.arange(NDEV, dtype=jnp.int32))
    return result.reshape(ROWS).astype(jnp.int32)


def block_scale(key, extent, pieces, smallest, largest):
    loudness = 1.0
    for axis_at, shards_of in pieces:
        draws = jax.random.uniform(jax.random.fold_in(jax.random.fold_in(key, 6), axis_at), (shards_of,), jnp.float32, smallest / len(pieces), largest / len(pieces))
        loudness = loudness * jnp.repeat(jnp.exp(draws), extent[axis_at] // shards_of).reshape((-1,) + (1,) * (len(extent) - 1 - axis_at))
    return loudness


def normal_values(stream_key, dims, scale, most, cuts=(), held_as=jnp.bfloat16):
    values = jax.random.normal(stream_key, dims, jnp.float32) * scale
    if len(cuts) > 0:
        values = block_scale(stream_key, dims, cuts, -0.22, 0.18) * values
    return jnp.clip(values, min=-most, max=most).astype(held_as)


def setup_inputs(seed: int = 0) -> dict:
    splits = jax.random.split(jax.random.key(seed), 5)
    return {
        "a_tiles": normal_values(splits[0], (ROWS, K, B, B), (K * B) ** -0.5, 0.15625, ((0, 128),)),
        "a_cols": draw_a_cols(jax.random.fold_in(splits[4], 71), 0),
        "p_tiles": normal_values(splits[2], (ROWS, B, B), B ** -0.5, 0.75, ((0, 128),)),
        "aggregate": draw_aggregate(jax.random.fold_in(splits[4], 71), 0),
    }


def reference(a_tiles, a_cols, p_tiles, aggregate):
    blocks_a = a_tiles.reshape(NDEV, ROW_DEV, K, B, B)
    blocks_c = a_cols.reshape(NDEV, ROW_DEV, K)

    def one_block(args):
        tiles, cols = args
        ghosts = p_tiles[cols]
        prod = jnp.einsum("rkab,rkbc->rac", tiles.astype(jnp.float32), ghosts.astype(jnp.float32))
        return prod.astype(jnp.bfloat16)

    ap_rows = lax.map(one_block, (blocks_a, blocks_c)).reshape(ROWS, B, B)
    partial_value = jnp.einsum("rba,rbc->rac", p_tiles.astype(jnp.float32), ap_rows.astype(jnp.float32))
    coarse = jax.ops.segment_sum(partial_value, aggregate, num_segments=NAGG)
    return ap_rows, coarse
```

```python
import functools

import jax
import jax.numpy as jnp
from jax import lax
from jax.experimental import pallas as pl
from jax.experimental.pallas import tpu as pltpu
from jax.sharding import PartitionSpec as P

AGG_DEV = 16
BOTH = ("px", "py")
BF = jnp.bfloat16
F32 = jnp.float32
VMEM_LIMIT = 24 * 2**20
ROWS16 = 16
SLOTS = 2
TAGS = 8
WHOLE = pl.BlockSpec(memory_space=pltpu.VMEM)
SCALARS = pl.BlockSpec(memory_space=pltpu.SMEM)
ANYWHERE = pl.BlockSpec(memory_space=pl.ANY)


def passed_along(x, axis, by):
    peers = lax.axis_size(axis)
    pairs = [(i, i + by) for i in range(peers) if 0 <= i + by < peers]
    return lax.ppermute(x, axis, pairs)


def params():
    return pltpu.CompilerParams(vmem_limit_bytes=VMEM_LIMIT)


def stacked(matrices):
    return jnp.swapaxes(jnp.stack([m.T for m in matrices]), 0, 1)


def pack_kernel(p_ref, out_ref):
    half = p_ref.shape[0] // 2
    for g in range(0, half, ROWS16):
        pairs = [
            jnp.concatenate([p_ref[g + i], p_ref[g + i + half]], axis=0) for i in range(ROWS16)
        ]
        out_ref[:, g : g + ROWS16, :] = stacked(pairs)


def pack_tiles(p_native):
    width, _, rows = p_native.shape
    return pl.pallas_call(
        pack_kernel,
        out_shape=jax.ShapeDtypeStruct((rows, width // 2, 2 * width), BF),
        compiler_params=params(),
        cost_estimate=pl.CostEstimate(flops=0, bytes_accessed=4 * 2**20, transcendentals=0),
        name="pack_tiles",
    )(p_native)


def turn_kernel(a_hbm, out_ref, a_ref, sems):
    blocks, width, _, rows = a_hbm.shape
    half = width // 2
    groups = width // ROWS16

    def fetch(k):
        return pltpu.make_async_copy(a_hbm.at[k], a_ref.at[k], sems.at[k])

    for k in range(blocks):
        fetch(k).start()

    def chunk(j, count):
        def group(g, carry):
            part = g // groups
            first = pl.multiple_of((g % groups) * ROWS16, ROWS16)
            from_b = pl.ds(pl.multiple_of(part * half, half), half)
            mats = []
            for i in range(ROWS16):
                x = a_ref[pl.ds(4 * j, count), first + i, from_b, :].reshape(count * half, rows)
                if count < 4:
                    x = jnp.concatenate([x, jnp.zeros(((4 - count) * half, rows), BF)], axis=0)
                mats.append(x)
            to = pl.ds(pl.multiple_of(part * width + first, ROWS16), ROWS16)
            out_ref[j, :, to, :] = stacked(mats)
            return carry

        lax.fori_loop(0, 2 * groups, group, 0, unroll=4)

    def full_chunk(j, carry):
        for i in range(4):
            fetch(4 * j + i).wait()
        chunk(j, 4)
        return carry

    full = blocks // 4
    lax.fori_loop(0, full, full_chunk, 0)
    for k in range(4 * full, blocks):
        fetch(k).wait()
    if blocks % 4:
        chunk(full, blocks % 4)


def turn_p_kernel(p_ref, pt_ref):
    half = p_ref.shape[0] // 2
    for g in range(0, half, ROWS16):
        low = jnp.swapaxes(p_ref[:, g : g + ROWS16, :], 0, 1)
        high = jnp.swapaxes(p_ref[:, g + half : g + half + ROWS16, :], 0, 1)
        pt_ref[:, g : g + ROWS16, :] = stacked(
            [jnp.concatenate([low[i], high[i]], axis=0) for i in range(ROWS16)]
        )


def turn_p(p_native):
    width, _, rows = p_native.shape
    return pl.pallas_call(
        turn_p_kernel,
        in_specs=[WHOLE],
        out_specs=WHOLE,
        out_shape=jax.ShapeDtypeStruct((rows, width // 2, 2 * width), BF),
        compiler_params=params(),
        cost_estimate=pl.CostEstimate(flops=0, bytes_accessed=4 * 2**20, transcendentals=0),
        name="turn_p",
    )(p_native)


def turn_blocks(a_native):
    blocks, width, _, rows = a_native.shape
    chunks = (blocks + 3) // 4
    half = width // 2
    return pl.pallas_call(
        turn_kernel,
        in_specs=[ANYWHERE],
        out_specs=WHOLE,
        out_shape=pltpu.VMEM((chunks, rows, 2 * width, 4 * half), BF),
        scratch_shapes=[pltpu.VMEM(a_native.shape, BF), pltpu.SemaphoreType.DMA((blocks,))],
        compiler_params=params(),
        cost_estimate=pl.CostEstimate(flops=0, bytes_accessed=40 * 2**20, transcendentals=0),
        name="turn_blocks",
    )(a_native)


def galerkin_kernel(
    idx_ref, pos_ref, tag_ref, a_ref, pt_ref, p0, p1, p2, p3, p4, ap_hbm, send_ref,
    ap_ref, pool, mixed, sems, ap_sem
):
    rows, half, wide = p0.shape
    blocks = idx_ref.shape[0]
    chunks = a_ref.shape[0]
    width = 2 * half
    group = mixed.shape[0]
    copies = [
        pltpu.make_async_copy(src, pool.at[pl.ds(i * rows, rows)], sems.at[i])
        for i, src in enumerate((p0, p1, p2, p3, p4))
    ]
    for copy in copies:
        copy.start()
    tiles_at = SLOTS * half
    send_ref[:, :tiles_at, :] = jnp.zeros((send_ref.shape[0], tiles_at, wide), BF)
    send_ref[:, tiles_at:, :] = tag_ref[...]
    for copy in copies:
        copy.wait()

    def keep(g):
        part = pl.ds(pl.multiple_of(g * group, group), group)
        return pltpu.make_async_copy(ap_ref.at[part], ap_hbm.at[part], ap_sem.at[g])

    left = lax.broadcasted_iota(jnp.int32, (width, wide), 1) < width
    none = jnp.zeros((half, wide), BF)

    def some_rows(g, carry):
        for i in range(group):
            r = g * group + i
            tiles = [pool[idx_ref[k, r]] for k in range(blocks)]
            ghosts = jnp.concatenate(tiles + [none] * (4 * chunks - blocks), axis=0)
            lhs = jnp.concatenate([a_ref[j, r] for j in range(chunks)], axis=1)
            prod = jnp.dot(lhs, ghosts, preferred_element_type=F32)
            mixed[i] = jnp.where(left, prod[:width], prod[width:])
        for i in range(group):
            r = g * group + i
            value = mixed[i]
            twice = value + pltpu.roll(value, width, 1)
            ap_ref[r] = twice.astype(BF)[:, :width]
            upper = jnp.where(left, twice, 0.0).astype(BF)
            lower = jnp.where(left, 0.0, twice).astype(BF)
            part = jnp.dot(
                pt_ref[r], jnp.concatenate([upper, lower], axis=0), preferred_element_type=F32
            )
            at = pos_ref[r]
            slot = pl.ds(pl.multiple_of((at % SLOTS) * half, half), half)
            send_ref[at // SLOTS, slot, :] = part.astype(BF)
        keep(g).start()
        return carry

    def kept(g, carry):
        keep(g).wait()
        return carry

    lax.fori_loop(0, rows // group, some_rows, 0)
    lax.fori_loop(0, rows // group, kept, 0)


def galerkin(index, position, tags, turned, p_turned, pieces):
    chunks, rows, wide, _ = turned.shape
    half = wide // 4
    width = 2 * half
    group = 16
    return pl.pallas_call(
        galerkin_kernel,
        in_specs=[SCALARS, SCALARS, WHOLE, WHOLE, WHOLE] + [ANYWHERE] * 5,
        out_specs=[pl.BlockSpec(memory_space=pltpu.HBM), WHOLE],
        out_shape=[
            pltpu.HBM((rows, width, width), BF),
            jax.ShapeDtypeStruct((tags.shape[0], SLOTS * half + TAGS, wide), BF),
        ],
        scratch_shapes=[
            pltpu.VMEM((rows, width, width), BF),
            pltpu.VMEM((5 * rows, half, wide), BF),
            pltpu.VMEM((group, width, wide), F32),
            pltpu.SemaphoreType.DMA((5,)),
            pltpu.SemaphoreType.DMA((rows // group,)),
        ],
        compiler_params=params(),
        cost_estimate=pl.CostEstimate(
            flops=2 * rows * wide * wide * chunks * wide, bytes_accessed=30 * 2**20, transcendentals=0
        ),
        name="galerkin",
    )(index, position, tags, pltpu.with_memory_space_constraint(turned, pltpu.VMEM), p_turned, *pieces)


def restore_kernel(ap_ref, out_ref):
    for g in range(0, ap_ref.shape[1], ROWS16):
        turned = jnp.swapaxes(ap_ref[:, g : g + ROWS16, :], 0, 1)
        for i in range(ROWS16):
            out_ref[g + i] = turned[i].T


def restore(ap):
    rows, width, _ = ap.shape
    return pl.pallas_call(
        restore_kernel,
        out_shape=jax.ShapeDtypeStruct((width, width, rows), BF),
        compiler_params=params(),
        cost_estimate=pl.CostEstimate(flops=0, bytes_accessed=8 * 2**20, transcendentals=0),
        name="restore",
    )(ap)


def sums_kernel(got_ref, out_ref):
    parts, height, wide = got_ref.shape
    half = wide // 4
    width = 2 * half
    tags = jnp.swapaxes(got_ref[:, SLOTS * half :, :], 0, 1)
    lane = lax.broadcasted_iota(jnp.int32, (parts, wide), 1) + 1
    chosen = [
        jnp.where(tags[s].astype(jnp.int32) == lane, 1.0, 0.0).T[:AGG_DEV].astype(BF)
        for s in range(SLOTS)
    ]
    chosen = jnp.concatenate(chosen, axis=1)
    for g in range(0, half, ROWS16):
        slots = [
            jnp.swapaxes(got_ref[:, s * half + g : s * half + g + ROWS16, :], 0, 1)
            for s in range(SLOTS)
        ]
        values = [
            jnp.dot(
                chosen,
                jnp.concatenate([slot[i] for slot in slots], axis=0),
                preferred_element_type=F32,
            )
            for i in range(ROWS16)
        ]
        value = jnp.swapaxes(jnp.stack(values), 0, 1)
        out_ref[:, g : g + ROWS16, :] = value[:, :, :width]
        out_ref[:, g + half : g + half + ROWS16, :] = value[:, :, width:]


def sums(got):
    parts, height, wide = got.shape
    width = wide // 2
    return pl.pallas_call(
        sums_kernel,
        in_specs=[WHOLE],
        out_specs=WHOLE,
        out_shape=jax.ShapeDtypeStruct((AGG_DEV, width, width), F32),
        compiler_params=params(),
        name="sums",
    )(got)


def shards(a_tiles, a_cols, p_tiles, aggregate):
    rows = p_tiles.shape[0]
    grid_x = lax.axis_size("px")
    grid_y = lax.axis_size("py")
    parts = grid_x * grid_y
    me_index = lax.axis_index("px") * grid_y + lax.axis_index("py")

    p_native = jnp.transpose(p_tiles, (1, 2, 0))
    tiles = pack_tiles(p_native)
    p_turned = turn_p(p_native)
    pieces = [tiles]
    for axis in ("py", "px"):
        for step in (1, -1):
            pieces.append(passed_along(tiles, axis, step))

    cols = a_cols.T
    delta = cols // rows - me_index
    code = jnp.where(
        delta == 0,
        0,
        jnp.where(delta == -1, 1, jnp.where(delta == 1, 2, jnp.where(delta == -grid_y, 3, 4))),
    )
    index = code * rows + cols % rows

    owner = aggregate // AGG_DEV
    order = jnp.arange(rows, dtype=jnp.int32)
    earlier = (owner[:, None] == owner[None, :]) & (order[None, :] < order[:, None])
    rank = jnp.sum(earlier.astype(jnp.int32), axis=1)
    position = owner * SLOTS + rank
    spots = jnp.arange(parts * SLOTS, dtype=jnp.int32)
    placing = position[:, None] == spots[None, :]
    label = jnp.sum(jnp.where(placing, (aggregate % AGG_DEV + 1)[:, None], 0), axis=0)
    label = jnp.pad(label.astype(BF).reshape(parts, SLOTS), ((0, 0), (0, TAGS - SLOTS)))
    tags = jnp.broadcast_to(label[:, :, None], (parts, TAGS, 2 * p_tiles.shape[1]))

    a_native = jnp.transpose(a_tiles, (1, 2, 3, 0))
    a_native, index, position, tags, p_turned = lax.optimization_barrier(
        (a_native, index, position, tags, p_turned)
    )
    turned = turn_blocks(a_native)
    ap, send = galerkin(index, position, tags, turned, p_turned, pieces)
    got = lax.all_to_all(send, BOTH, split_axis=0, concat_axis=0, tiled=True)
    ap_native = restore(ap)
    coarse = sums(got)
    return (jnp.transpose(ap_native, (2, 0, 1)), coarse)


def solution(mesh):
    return jax.shard_map(
        shards,
        mesh=mesh,
        in_specs=(
            P(BOTH, None, None, None),
            P(BOTH, None),
            P(BOTH, None, None),
            P(BOTH),
        ),
        out_specs=(P(BOTH, None, None), P(BOTH, None, None)),
        check_vma=False,
    )
```

```python
import functools

import jax
import jax.numpy as jnp
from jax import lax
from jax.experimental import pallas as pl
from jax.experimental.pallas import tpu as pltpu
from jax.sharding import PartitionSpec as P

AGG_DEV = 16
BOTH = ("px", "py")
BF = jnp.bfloat16
F32 = jnp.float32
VMEM_LIMIT = 24 * 2**20
ROWS16 = 16
SLOTS = 2
TAGS = 8
WHOLE = pl.BlockSpec(memory_space=pltpu.VMEM)
SCALARS = pl.BlockSpec(memory_space=pltpu.SMEM)
ANYWHERE = pl.BlockSpec(memory_space=pl.ANY)


def passed_along(x, axis, by):
    peers = lax.axis_size(axis)
    pairs = [(i, i + by) for i in range(peers) if 0 <= i + by < peers]
    return lax.ppermute(x, axis, pairs)


def params():
    return pltpu.CompilerParams(vmem_limit_bytes=VMEM_LIMIT)


def stacked(matrices):
    return jnp.swapaxes(jnp.stack([m.T for m in matrices]), 0, 1)


def packed(p_ref, g):
    half = p_ref.shape[0] // 2
    return stacked(
        [jnp.concatenate([p_ref[g + i], p_ref[g + i + half]], axis=0) for i in range(ROWS16)]
    )


def turn_kernel(a_hbm, out_ref, a_ref, sems):
    blocks, width, _, rows = a_hbm.shape
    half = width // 2
    groups = width // ROWS16

    def fetch(k):
        return pltpu.make_async_copy(a_hbm.at[k], a_ref.at[k], sems.at[k])

    for k in range(blocks):
        fetch(k).start()

    def chunk(j, count):
        def group(g, carry):
            part = g // groups
            first = pl.multiple_of((g % groups) * ROWS16, ROWS16)
            from_b = pl.ds(pl.multiple_of(part * half, half), half)
            mats = []
            for i in range(ROWS16):
                x = a_ref[pl.ds(4 * j, count), first + i, from_b, :].reshape(count * half, rows)
                if count < 4:
                    x = jnp.concatenate([x, jnp.zeros(((4 - count) * half, rows), BF)], axis=0)
                mats.append(x)
            to = pl.ds(pl.multiple_of(part * width + first, ROWS16), ROWS16)
            out_ref[j, :, to, :] = stacked(mats)
            return carry

        lax.fori_loop(0, 2 * groups, group, 0, unroll=8)

    def full_chunk(j, carry):
        for i in range(4):
            fetch(4 * j + i).wait()
        chunk(j, 4)
        return carry

    full = blocks // 4
    lax.fori_loop(0, full, full_chunk, 0)
    for k in range(4 * full, blocks):
        fetch(k).wait()
    if blocks % 4:
        chunk(full, blocks % 4)


def own_kernel(p_ref, own_ref):
    half = p_ref.shape[0] // 2
    for g in range(0, half, ROWS16):
        own_ref[:, g : g + ROWS16, :] = packed(p_ref, g)
        low = jnp.swapaxes(p_ref[:, g : g + ROWS16, :], 0, 1)
        high = jnp.swapaxes(p_ref[:, g + half : g + half + ROWS16, :], 0, 1)
        own_ref[:, g + half : g + half + ROWS16, :] = stacked(
            [jnp.concatenate([low[i], high[i]], axis=0) for i in range(ROWS16)]
        )


def own_tiles(p_native):
    width, _, rows = p_native.shape
    return pl.pallas_call(
        own_kernel,
        in_specs=[WHOLE],
        out_specs=WHOLE,
        out_shape=jax.ShapeDtypeStruct((rows, width, 2 * width), BF),
        compiler_params=params(),
        cost_estimate=pl.CostEstimate(flops=0, bytes_accessed=4 * 2**20, transcendentals=0),
        name="own_tiles",
    )(p_native)


def turn_blocks(a_native):
    blocks, width, _, rows = a_native.shape
    chunks = (blocks + 3) // 4
    half = width // 2
    return pl.pallas_call(
        turn_kernel,
        in_specs=[ANYWHERE],
        out_specs=WHOLE,
        out_shape=pltpu.VMEM((chunks, rows, 2 * width, 4 * half), BF),
        scratch_shapes=[pltpu.VMEM(a_native.shape, BF), pltpu.SemaphoreType.DMA((blocks,))],
        compiler_params=params(),
        cost_estimate=pl.CostEstimate(flops=0, bytes_accessed=40 * 2**20, transcendentals=0),
        name="turn_blocks",
    )(a_native)


def galerkin_kernel(
    idx_ref, pos_ref, tag_ref, a_ref, own_ref, p1, p2, p3, p4, ap_hbm, send_hbm,
    ap_ref, send_ref, pool, natives, mixed, sems, ap_sem, send_sem
):
    rows, width, wide = own_ref.shape
    half = width // 2
    blocks = idx_ref.shape[0]
    chunks = a_ref.shape[0]
    group = mixed.shape[0]
    others = (p1, p2, p3, p4)
    copies = [pltpu.make_async_copy(own_ref.at[:, pl.ds(0, half)], pool.at[pl.ds(0, rows)], sems.at[0])]
    for i, src in enumerate(others):
        copies.append(pltpu.make_async_copy(src, natives.at[i], sems.at[i + 1]))
    for copy in copies:
        copy.start()
    tiles_at = SLOTS * half
    send_ref[:, :tiles_at, :] = jnp.zeros((send_ref.shape[0], tiles_at, wide), BF)
    send_ref[:, tiles_at:, :] = tag_ref[...]
    for i in range(len(others)):
        copies[i + 1].wait()
        for g in range(0, half, ROWS16):
            pool[(i + 1) * rows : (i + 2) * rows, g : g + ROWS16, :] = packed(natives.at[i], g)
    copies[0].wait()

    def keep(g):
        part = pl.ds(pl.multiple_of(g * group, group), group)
        return pltpu.make_async_copy(ap_ref.at[part], ap_hbm.at[part], ap_sem.at[g])

    left = lax.broadcasted_iota(jnp.int32, (width, wide), 1) < width
    none = jnp.zeros((half, wide), BF)

    def some_rows(g, carry):
        for i in range(group):
            r = g * group + i
            tiles = [pool[idx_ref[k, r]] for k in range(blocks)]
            ghosts = jnp.concatenate(tiles + [none] * (4 * chunks - blocks), axis=0)
            lhs = jnp.concatenate([a_ref[j, r] for j in range(chunks)], axis=1)
            prod = jnp.dot(lhs, ghosts, preferred_element_type=F32)
            mixed[i] = jnp.where(left, prod[:width], prod[width:])
        for i in range(group):
            r = g * group + i
            value = mixed[i]
            twice = value + pltpu.roll(value, width, 1)
            ap_ref[r] = twice.astype(BF)[:, :width]
            upper = jnp.where(left, twice, 0.0).astype(BF)
            lower = jnp.where(left, 0.0, twice).astype(BF)
            part = jnp.dot(
                own_ref[r, half:, :], jnp.concatenate([upper, lower], axis=0), preferred_element_type=F32
            )
            at = pos_ref[r]
            slot = pl.ds(pl.multiple_of((at % SLOTS) * half, half), half)
            send_ref[at // SLOTS, slot, :] = part.astype(BF)
        keep(g).start()
        return carry

    def kept(g, carry):
        keep(g).wait()
        return carry

    lax.fori_loop(0, rows // group, some_rows, 0)
    send = pltpu.make_async_copy(send_ref, send_hbm, send_sem)
    send.start()
    send.wait()
    lax.fori_loop(0, rows // group, kept, 0)


def galerkin(index, position, tags, turned, own, pieces):
    chunks, rows, wide, _ = turned.shape
    half = wide // 4
    width = 2 * half
    group = 32
    return pl.pallas_call(
        galerkin_kernel,
        in_specs=[SCALARS, SCALARS, WHOLE, WHOLE, WHOLE] + [ANYWHERE] * 4,
        out_specs=[pl.BlockSpec(memory_space=pltpu.HBM)] * 2,
        out_shape=[
            pltpu.HBM((rows, width, width), BF),
            pltpu.HBM((tags.shape[0], SLOTS * half + TAGS, wide), BF),
        ],
        scratch_shapes=[
            pltpu.VMEM((rows, width, width), BF),
            pltpu.VMEM((tags.shape[0], SLOTS * half + TAGS, wide), BF),
            pltpu.VMEM((5 * rows, half, wide), BF),
            pltpu.VMEM((4, width, width, rows), BF),
            pltpu.VMEM((group, width, wide), F32),
            pltpu.SemaphoreType.DMA((5,)),
            pltpu.SemaphoreType.DMA((rows // group,)),
            pltpu.SemaphoreType.DMA,
        ],
        compiler_params=params(),
        cost_estimate=pl.CostEstimate(
            flops=2 * rows * wide * wide * chunks * wide, bytes_accessed=30 * 2**20, transcendentals=0
        ),
        name="galerkin",
    )(index, position, tags, pltpu.with_memory_space_constraint(turned, pltpu.VMEM), own, *pieces)


def restore_kernel(ap_ref, out_ref):
    for g in range(0, ap_ref.shape[1], ROWS16):
        turned = jnp.swapaxes(ap_ref[:, g : g + ROWS16, :], 0, 1)
        for i in range(ROWS16):
            out_ref[g + i] = turned[i].T


def restore(ap):
    rows, width, _ = ap.shape
    return pl.pallas_call(
        restore_kernel,
        out_shape=jax.ShapeDtypeStruct((width, width, rows), BF),
        compiler_params=params(),
        cost_estimate=pl.CostEstimate(flops=0, bytes_accessed=8 * 2**20, transcendentals=0),
        name="restore",
    )(ap)


def sums_kernel(got_ref, out_ref):
    parts, height, wide = got_ref.shape
    half = wide // 4
    width = 2 * half
    tags = jnp.swapaxes(got_ref[:, SLOTS * half :, :], 0, 1)
    lane = lax.broadcasted_iota(jnp.int32, (parts, wide), 1) + 1
    chosen = [
        jnp.where(tags[s].astype(jnp.int32) == lane, 1.0, 0.0).T[:AGG_DEV].astype(BF)
        for s in range(SLOTS)
    ]
    chosen = jnp.concatenate(chosen, axis=1)
    for g in range(0, half, ROWS16):
        slots = [
            jnp.swapaxes(got_ref[:, s * half + g : s * half + g + ROWS16, :], 0, 1)
            for s in range(SLOTS)
        ]
        values = [
            jnp.dot(
                chosen,
                jnp.concatenate([slot[i] for slot in slots], axis=0),
                preferred_element_type=F32,
            )
            for i in range(ROWS16)
        ]
        value = jnp.swapaxes(jnp.stack(values), 0, 1)
        out_ref[:, g : g + ROWS16, :] = value[:, :, :width]
        out_ref[:, g + half : g + half + ROWS16, :] = value[:, :, width:]


def sums(got):
    parts, height, wide = got.shape
    width = wide // 2
    return pl.pallas_call(
        sums_kernel,
        in_specs=[WHOLE],
        out_specs=WHOLE,
        out_shape=jax.ShapeDtypeStruct((AGG_DEV, width, width), F32),
        compiler_params=params(),
        name="sums",
    )(got)


def shards(a_tiles, a_cols, p_tiles, aggregate):
    rows = p_tiles.shape[0]
    grid_x = lax.axis_size("px")
    grid_y = lax.axis_size("py")
    parts = grid_x * grid_y
    me_index = lax.axis_index("px") * grid_y + lax.axis_index("py")

    p_native = jnp.transpose(p_tiles, (1, 2, 0))
    own = own_tiles(p_native)
    pieces = []
    for axis in ("py", "px"):
        for step in (1, -1):
            pieces.append(passed_along(p_native, axis, step))

    cols = a_cols.T
    delta = cols // rows - me_index
    code = jnp.where(
        delta == 0,
        0,
        jnp.where(delta == -1, 1, jnp.where(delta == 1, 2, jnp.where(delta == -grid_y, 3, 4))),
    )
    index = code * rows + cols % rows

    owner = aggregate // AGG_DEV
    order = jnp.arange(rows, dtype=jnp.int32)
    earlier = (owner[:, None] == owner[None, :]) & (order[None, :] < order[:, None])
    rank = jnp.sum(earlier.astype(jnp.int32), axis=1)
    position = owner * SLOTS + rank
    spots = jnp.arange(parts * SLOTS, dtype=jnp.int32)
    placing = position[:, None] == spots[None, :]
    label = jnp.sum(jnp.where(placing, (aggregate % AGG_DEV + 1)[:, None], 0), axis=0)
    label = jnp.pad(label.astype(BF).reshape(parts, SLOTS), ((0, 0), (0, TAGS - SLOTS)))
    tags = jnp.broadcast_to(label[:, :, None], (parts, TAGS, 2 * p_tiles.shape[1]))

    a_native = jnp.transpose(a_tiles, (1, 2, 3, 0))
    a_native, index, position, tags, own = lax.optimization_barrier(
        (a_native, index, position, tags, own)
    )
    turned = turn_blocks(a_native)
    ap, send = galerkin(index, position, tags, turned, own, pieces)
    got = lax.all_to_all(send, BOTH, split_axis=0, concat_axis=0, tiled=True)
    ap_native = restore(ap)
    coarse = sums(got)
    return (jnp.transpose(ap_native, (2, 0, 1)), coarse)


def solution(mesh):
    return jax.shard_map(
        shards,
        mesh=mesh,
        in_specs=(
            P(BOTH, None, None, None),
            P(BOTH, None),
            P(BOTH, None, None),
            P(BOTH),
        ),
        out_specs=(P(BOTH, None, None), P(BOTH, None, None)),
        check_vma=False,
    )
```

```python
import functools

import jax
import jax.numpy as jnp
from jax import lax
from jax.experimental import pallas as pl
from jax.experimental.pallas import tpu as pltpu
from jax.sharding import PartitionSpec as P

AGG_DEV = 16
BOTH = ("px", "py")
BF = jnp.bfloat16
F32 = jnp.float32
VMEM_LIMIT = 24 * 2**20
ROWS16 = 16
SLOTS = 2
TAGS = 8
WHOLE = pl.BlockSpec(memory_space=pltpu.VMEM)
SCALARS = pl.BlockSpec(memory_space=pltpu.SMEM)
ANYWHERE = pl.BlockSpec(memory_space=pl.ANY)


def passed_along(x, axis, by):
    peers = lax.axis_size(axis)
    pairs = [(i, i + by) for i in range(peers) if 0 <= i + by < peers]
    return lax.ppermute(x, axis, pairs)


def params():
    return pltpu.CompilerParams(vmem_limit_bytes=VMEM_LIMIT)


def stacked(matrices):
    return jnp.swapaxes(jnp.stack([m.T for m in matrices]), 0, 1)


def packed(p_ref, g):
    half = p_ref.shape[0] // 2
    return stacked(
        [jnp.concatenate([p_ref[g + i], p_ref[g + i + half]], axis=0) for i in range(ROWS16)]
    )


def turn_kernel(a_hbm, out_ref, a_ref, sems):
    blocks, width, _, rows = a_hbm.shape
    half = width // 2
    groups = width // ROWS16

    def fetch(k):
        return pltpu.make_async_copy(a_hbm.at[k], a_ref.at[k], sems.at[k])

    for k in range(blocks):
        fetch(k).start()

    def chunk(j, count):
        def group(g, carry):
            part = g // groups
            first = pl.multiple_of((g % groups) * ROWS16, ROWS16)
            from_b = pl.ds(pl.multiple_of(part * half, half), half)
            mats = []
            for i in range(ROWS16):
                x = a_ref[pl.ds(4 * j, count), first + i, from_b, :].reshape(count * half, rows)
                if count < 4:
                    x = jnp.concatenate([x, jnp.zeros(((4 - count) * half, rows), BF)], axis=0)
                mats.append(x)
            to = pl.ds(pl.multiple_of(part * width + first, ROWS16), ROWS16)
            out_ref[j, :, to, :] = stacked(mats)
            return carry

        lax.fori_loop(0, 2 * groups, group, 0, unroll=8)

    def full_chunk(j, carry):
        for i in range(4):
            fetch(4 * j + i).wait()
        chunk(j, 4)
        return carry

    full = blocks // 4
    lax.fori_loop(0, full, full_chunk, 0)
    for k in range(4 * full, blocks):
        fetch(k).wait()
    if blocks % 4:
        chunk(full, blocks % 4)


def own_kernel(p_ref, own_ref):
    half = p_ref.shape[0] // 2
    for g in range(0, half, ROWS16):
        own_ref[:, g : g + ROWS16, :] = packed(p_ref, g)
        low = jnp.swapaxes(p_ref[:, g : g + ROWS16, :], 0, 1)
        high = jnp.swapaxes(p_ref[:, g + half : g + half + ROWS16, :], 0, 1)
        own_ref[:, g + half : g + half + ROWS16, :] = stacked(
            [jnp.concatenate([low[i], high[i]], axis=0) for i in range(ROWS16)]
        )


def own_tiles(p_native):
    width, _, rows = p_native.shape
    return pl.pallas_call(
        own_kernel,
        in_specs=[WHOLE],
        out_specs=WHOLE,
        out_shape=jax.ShapeDtypeStruct((rows, width, 2 * width), BF),
        compiler_params=params(),
        cost_estimate=pl.CostEstimate(flops=0, bytes_accessed=4 * 2**20, transcendentals=0),
        name="own_tiles",
    )(p_native)


def turn_blocks(a_native):
    blocks, width, _, rows = a_native.shape
    chunks = (blocks + 3) // 4
    half = width // 2
    return pl.pallas_call(
        turn_kernel,
        in_specs=[ANYWHERE],
        out_specs=WHOLE,
        out_shape=pltpu.VMEM((chunks, rows, 2 * width, 4 * half), BF),
        scratch_shapes=[pltpu.VMEM(a_native.shape, BF), pltpu.SemaphoreType.DMA((blocks,))],
        compiler_params=params(),
        cost_estimate=pl.CostEstimate(flops=0, bytes_accessed=40 * 2**20, transcendentals=0),
        name="turn_blocks",
    )(a_native)


def galerkin_kernel(
    idx_ref, pos_ref, tag_ref, a_ref, own_ref, p1, p2, p3, p4, ap_hbm, send_hbm,
    ap_ref, send_ref, pool, natives, mixed, sems, ap_sem, send_sem
):
    rows, width, wide = own_ref.shape
    half = width // 2
    blocks = idx_ref.shape[0]
    chunks = a_ref.shape[0]
    group = mixed.shape[0]
    others = (p1, p2, p3, p4)
    copies = [pltpu.make_async_copy(own_ref.at[:, pl.ds(0, half)], pool.at[pl.ds(0, rows)], sems.at[0])]
    for i, src in enumerate(others):
        copies.append(pltpu.make_async_copy(src, natives.at[i], sems.at[i + 1]))
    for copy in reversed(copies):
        copy.start()
    tiles_at = SLOTS * half
    send_ref[:, :tiles_at, :] = jnp.zeros((send_ref.shape[0], tiles_at, wide), BF)
    send_ref[:, tiles_at:, :] = tag_ref[...]
    for i in reversed(range(len(others))):
        copies[i + 1].wait()
        for g in range(0, half, ROWS16):
            pool[(i + 1) * rows : (i + 2) * rows, g : g + ROWS16, :] = packed(natives.at[i], g)
    copies[0].wait()

    def keep(g):
        part = pl.ds(pl.multiple_of(g * group, group), group)
        return pltpu.make_async_copy(ap_ref.at[part], ap_hbm.at[part], ap_sem.at[g])

    left = lax.broadcasted_iota(jnp.int32, (width, wide), 1) < width
    none = jnp.zeros((half, wide), BF)

    def some_rows(g, carry):
        for i in range(group):
            r = g * group + i
            tiles = [pool[idx_ref[k, r]] for k in range(blocks)]
            ghosts = jnp.concatenate(tiles + [none] * (4 * chunks - blocks), axis=0)
            lhs = jnp.concatenate([a_ref[j, r] for j in range(chunks)], axis=1)
            prod = jnp.dot(lhs, ghosts, preferred_element_type=F32)
            mixed[i] = jnp.where(left, prod[:width], prod[width:])
        for i in range(group):
            r = g * group + i
            value = mixed[i]
            twice = value + pltpu.roll(value, width, 1)
            ap_ref[r] = twice.astype(BF)[:, :width]
            upper = jnp.where(left, twice, 0.0).astype(BF)
            lower = jnp.where(left, 0.0, twice).astype(BF)
            part = jnp.dot(
                own_ref[r, half:, :], jnp.concatenate([upper, lower], axis=0), preferred_element_type=F32
            )
            at = pos_ref[r]
            slot = pl.ds(pl.multiple_of((at % SLOTS) * half, half), half)
            send_ref[at // SLOTS, slot, :] = part.astype(BF)
        keep(g).start()
        return carry

    def kept(g, carry):
        keep(g).wait()
        return carry

    lax.fori_loop(0, rows // group, some_rows, 0)
    send = pltpu.make_async_copy(send_ref, send_hbm, send_sem)
    send.start()
    send.wait()
    lax.fori_loop(0, rows // group, kept, 0)


def galerkin(index, position, tags, turned, own, pieces):
    chunks, rows, wide, _ = turned.shape
    half = wide // 4
    width = 2 * half
    group = 64
    return pl.pallas_call(
        galerkin_kernel,
        in_specs=[SCALARS, SCALARS, WHOLE, WHOLE, WHOLE] + [ANYWHERE] * 4,
        out_specs=[pl.BlockSpec(memory_space=pltpu.HBM)] * 2,
        out_shape=[
            pltpu.HBM((rows, width, width), BF),
            pltpu.HBM((tags.shape[0], SLOTS * half + TAGS, wide), BF),
        ],
        scratch_shapes=[
            pltpu.VMEM((rows, width, width), BF),
            pltpu.VMEM((tags.shape[0], SLOTS * half + TAGS, wide), BF),
            pltpu.VMEM((5 * rows, half, wide), BF),
            pltpu.VMEM((4, width, width, rows), BF),
            pltpu.VMEM((group, width, wide), F32),
            pltpu.SemaphoreType.DMA((5,)),
            pltpu.SemaphoreType.DMA((rows // group,)),
            pltpu.SemaphoreType.DMA,
        ],
        compiler_params=params(),
        cost_estimate=pl.CostEstimate(
            flops=2 * rows * wide * wide * chunks * wide, bytes_accessed=30 * 2**20, transcendentals=0
        ),
        name="galerkin",
    )(index, position, tags, pltpu.with_memory_space_constraint(turned, pltpu.VMEM), own, *pieces)


def restore_kernel(ap_ref, out_ref):
    for g in range(0, ap_ref.shape[1], ROWS16):
        turned = jnp.swapaxes(ap_ref[:, g : g + ROWS16, :], 0, 1)
        for i in range(ROWS16):
            out_ref[g + i] = turned[i].T


def restore(ap):
    rows, width, _ = ap.shape
    return pl.pallas_call(
        restore_kernel,
        out_shape=jax.ShapeDtypeStruct((width, width, rows), BF),
        compiler_params=params(),
        cost_estimate=pl.CostEstimate(flops=0, bytes_accessed=8 * 2**20, transcendentals=0),
        name="restore",
    )(ap)


def sums_kernel(got_ref, out_ref):
    parts, height, wide = got_ref.shape
    half = wide // 4
    width = 2 * half
    tags = jnp.swapaxes(got_ref[:, SLOTS * half :, :], 0, 1)
    lane = lax.broadcasted_iota(jnp.int32, (parts, wide), 1) + 1
    chosen = [
        jnp.where(tags[s].astype(jnp.int32) == lane, 1.0, 0.0).T[:AGG_DEV].astype(BF)
        for s in range(SLOTS)
    ]
    chosen = jnp.concatenate(chosen, axis=1)
    for g in range(0, half, ROWS16):
        slots = [
            jnp.swapaxes(got_ref[:, s * half + g : s * half + g + ROWS16, :], 0, 1)
            for s in range(SLOTS)
        ]
        values = [
            jnp.dot(
                chosen,
                jnp.concatenate([slot[i] for slot in slots], axis=0),
                preferred_element_type=F32,
            )
            for i in range(ROWS16)
        ]
        value = jnp.swapaxes(jnp.stack(values), 0, 1)
        out_ref[:, g : g + ROWS16, :] = value[:, :, :width]
        out_ref[:, g + half : g + half + ROWS16, :] = value[:, :, width:]


def sums(got):
    parts, height, wide = got.shape
    width = wide // 2
    return pl.pallas_call(
        sums_kernel,
        in_specs=[WHOLE],
        out_specs=WHOLE,
        out_shape=jax.ShapeDtypeStruct((AGG_DEV, width, width), F32),
        compiler_params=params(),
        name="sums",
    )(got)


def shards(a_tiles, a_cols, p_tiles, aggregate):
    rows = p_tiles.shape[0]
    grid_x = lax.axis_size("px")
    grid_y = lax.axis_size("py")
    parts = grid_x * grid_y
    me_index = lax.axis_index("px") * grid_y + lax.axis_index("py")

    p_native = jnp.transpose(p_tiles, (1, 2, 0))
    own = own_tiles(p_native)
    pieces = []
    for axis in ("py", "px"):
        for step in (1, -1):
            pieces.append(passed_along(p_native, axis, step))

    cols = a_cols.T
    delta = cols // rows - me_index
    code = jnp.where(
        delta == 0,
        0,
        jnp.where(delta == -1, 1, jnp.where(delta == 1, 2, jnp.where(delta == -grid_y, 3, 4))),
    )
    index = code * rows + cols % rows

    owner = aggregate // AGG_DEV
    order = jnp.arange(rows, dtype=jnp.int32)
    earlier = (owner[:, None] == owner[None, :]) & (order[None, :] < order[:, None])
    rank = jnp.sum(earlier.astype(jnp.int32), axis=1)
    position = owner * SLOTS + rank
    spots = jnp.arange(parts * SLOTS, dtype=jnp.int32)
    placing = position[:, None] == spots[None, :]
    label = jnp.sum(jnp.where(placing, (aggregate % AGG_DEV + 1)[:, None], 0), axis=0)
    label = jnp.pad(label.astype(BF).reshape(parts, SLOTS), ((0, 0), (0, TAGS - SLOTS)))
    tags = jnp.broadcast_to(label[:, :, None], (parts, TAGS, 2 * p_tiles.shape[1]))

    a_native = jnp.transpose(a_tiles, (1, 2, 3, 0))
    a_native, index, position, tags, own = lax.optimization_barrier(
        (a_native, index, position, tags, own)
    )
    turned = turn_blocks(a_native)
    ap, send = galerkin(index, position, tags, turned, own, pieces)
    got = lax.all_to_all(send, BOTH, split_axis=0, concat_axis=0, tiled=True)
    ap_native = restore(ap)
    coarse = sums(got)
    return (jnp.transpose(ap_native, (2, 0, 1)), coarse)


def solution(mesh):
    return jax.shard_map(
        shards,
        mesh=mesh,
        in_specs=(
            P(BOTH, None, None, None),
            P(BOTH, None),
            P(BOTH, None, None),
            P(BOTH),
        ),
        out_specs=(P(BOTH, None, None), P(BOTH, None, None)),
        check_vma=False,
    )
```

```python
import functools

import jax
import jax.numpy as jnp
from jax import lax
from jax.experimental import pallas as pl
from jax.experimental.pallas import tpu as pltpu
from jax.sharding import PartitionSpec as P

AGG_DEV = 16
BOTH = ("px", "py")
BF = jnp.bfloat16
F32 = jnp.float32
VMEM_LIMIT = 24 * 2**20
ROWS16 = 16
SLOTS = 2
TAGS = 8
WHOLE = pl.BlockSpec(memory_space=pltpu.VMEM)
SCALARS = pl.BlockSpec(memory_space=pltpu.SMEM)
ANYWHERE = pl.BlockSpec(memory_space=pl.ANY)


def passed_along(x, axis, by):
    peers = lax.axis_size(axis)
    pairs = [(i, i + by) for i in range(peers) if 0 <= i + by < peers]
    return lax.ppermute(x, axis, pairs)


def params():
    return pltpu.CompilerParams(vmem_limit_bytes=VMEM_LIMIT)


def stacked(matrices):
    return jnp.swapaxes(jnp.stack([m.T for m in matrices]), 0, 1)


def packed(p_ref, g):
    half = p_ref.shape[0] // 2
    return stacked(
        [jnp.concatenate([p_ref[g + i], p_ref[g + i + half]], axis=0) for i in range(ROWS16)]
    )


def turn_kernel(a_hbm, out_ref, a_ref, sems):
    blocks, width, _, rows = a_hbm.shape
    half = width // 2
    groups = width // ROWS16

    def fetch(k):
        return pltpu.make_async_copy(a_hbm.at[k], a_ref.at[k], sems.at[k])

    for k in range(blocks):
        fetch(k).start()

    def chunk(j, count):
        def group(g, carry):
            part = g // groups
            first = pl.multiple_of((g % groups) * ROWS16, ROWS16)
            from_b = pl.ds(pl.multiple_of(part * half, half), half)
            mats = []
            for i in range(ROWS16):
                x = a_ref[pl.ds(4 * j, count), first + i, from_b, :].reshape(count * half, rows)
                if count < 4:
                    x = jnp.concatenate([x, jnp.zeros(((4 - count) * half, rows), BF)], axis=0)
                mats.append(x)
            to = pl.ds(pl.multiple_of(part * width + first, ROWS16), ROWS16)
            out_ref[j, :, to, :] = stacked(mats)
            return carry

        lax.fori_loop(0, 2 * groups, group, 0, unroll=8)

    def full_chunk(j, carry):
        for i in range(4):
            fetch(4 * j + i).wait()
        chunk(j, 4)
        return carry

    full = blocks // 4
    lax.fori_loop(0, full, full_chunk, 0)
    for k in range(4 * full, blocks):
        fetch(k).wait()
    if blocks % 4:
        chunk(full, blocks % 4)


def own_kernel(p_ref, own_ref):
    half = p_ref.shape[0] // 2
    for g in range(0, half, ROWS16):
        own_ref[:, g : g + ROWS16, :] = packed(p_ref, g)
        low = jnp.swapaxes(p_ref[:, g : g + ROWS16, :], 0, 1)
        high = jnp.swapaxes(p_ref[:, g + half : g + half + ROWS16, :], 0, 1)
        own_ref[:, g + half : g + half + ROWS16, :] = stacked(
            [jnp.concatenate([low[i], high[i]], axis=0) for i in range(ROWS16)]
        )


def own_tiles(p_native):
    width, _, rows = p_native.shape
    return pl.pallas_call(
        own_kernel,
        in_specs=[WHOLE],
        out_specs=WHOLE,
        out_shape=jax.ShapeDtypeStruct((rows, width, 2 * width), BF),
        compiler_params=params(),
        cost_estimate=pl.CostEstimate(flops=0, bytes_accessed=4 * 2**20, transcendentals=0),
        name="own_tiles",
    )(p_native)


def turn_blocks(a_native):
    blocks, width, _, rows = a_native.shape
    chunks = (blocks + 3) // 4
    half = width // 2
    return pl.pallas_call(
        turn_kernel,
        in_specs=[ANYWHERE],
        out_specs=WHOLE,
        out_shape=pltpu.VMEM((chunks, rows, 2 * width, 4 * half), BF),
        scratch_shapes=[pltpu.VMEM(a_native.shape, BF), pltpu.SemaphoreType.DMA((blocks,))],
        compiler_params=params(),
        cost_estimate=pl.CostEstimate(flops=0, bytes_accessed=40 * 2**20, transcendentals=0),
        name="turn_blocks",
    )(a_native)


def galerkin_kernel(
    idx_ref, pos_ref, tag_ref, a_ref, own_ref, p1, p2, p3, p4, ap_hbm, send_hbm,
    ap_ref, send_ref, pool, natives, mixed, sems, ap_sem, send_sem
):
    rows, width, wide = own_ref.shape
    half = width // 2
    blocks = idx_ref.shape[0]
    chunks = a_ref.shape[0]
    group = mixed.shape[0]
    others = (p1, p2, p3, p4)
    copies = [pltpu.make_async_copy(own_ref.at[:, pl.ds(0, half)], pool.at[pl.ds(0, rows)], sems.at[0])]
    for i, src in enumerate(others):
        copies.append(pltpu.make_async_copy(src, natives.at[i], sems.at[i + 1]))
    for copy in reversed(copies):
        copy.start()
    tiles_at = SLOTS * half
    send_ref[:, :tiles_at, :] = jnp.zeros((send_ref.shape[0], tiles_at, wide), BF)
    send_ref[:, tiles_at:, :] = tag_ref[...]
    for i in reversed(range(len(others))):
        copies[i + 1].wait()
        for g in range(0, half, ROWS16):
            pool[(i + 1) * rows : (i + 2) * rows, g : g + ROWS16, :] = packed(natives.at[i], g)
    copies[0].wait()

    def keep(g):
        part = pl.ds(pl.multiple_of(g * group, group), group)
        return pltpu.make_async_copy(ap_ref.at[part], ap_hbm.at[part], ap_sem.at[g])

    left = lax.broadcasted_iota(jnp.int32, (width, wide), 1) < width
    none = jnp.zeros((half, wide), BF)

    def some_rows(g, carry):
        for i in range(group):
            r = g * group + i
            tiles = [pool[idx_ref[k, r]] for k in range(blocks)]
            ghosts = jnp.concatenate(tiles + [none] * (4 * chunks - blocks), axis=0)
            lhs = jnp.concatenate([a_ref[j, r] for j in range(chunks)], axis=1)
            prod = jnp.dot(lhs, ghosts, preferred_element_type=F32)
            mixed[i] = jnp.where(left, prod[:width], prod[width:])
        for i in range(group):
            r = g * group + i
            value = mixed[i]
            twice = (value + pltpu.roll(value, width, 1)).astype(BF)
            ap_ref[r] = twice[:, :width]
            upper = jnp.where(left, twice, jnp.zeros_like(twice))
            lower = jnp.where(left, jnp.zeros_like(twice), twice)
            part = jnp.dot(
                own_ref[r, half:, :], jnp.concatenate([upper, lower], axis=0), preferred_element_type=F32
            )
            at = pos_ref[r]
            slot = pl.ds(pl.multiple_of((at % SLOTS) * half, half), half)
            send_ref[at // SLOTS, slot, :] = part.astype(BF)
        keep(g).start()
        return carry

    def kept(g, carry):
        keep(g).wait()
        return carry

    lax.fori_loop(0, rows // group, some_rows, 0)
    send = pltpu.make_async_copy(send_ref, send_hbm, send_sem)
    send.start()
    send.wait()
    lax.fori_loop(0, rows // group, kept, 0)


def galerkin(index, position, tags, turned, own, pieces):
    chunks, rows, wide, _ = turned.shape
    half = wide // 4
    width = 2 * half
    group = 64
    return pl.pallas_call(
        galerkin_kernel,
        in_specs=[SCALARS, SCALARS, WHOLE, WHOLE, WHOLE] + [ANYWHERE] * 4,
        out_specs=[pl.BlockSpec(memory_space=pltpu.HBM)] * 2,
        out_shape=[
            pltpu.HBM((rows, width, width), BF),
            pltpu.HBM((tags.shape[0], SLOTS * half + TAGS, wide), BF),
        ],
        scratch_shapes=[
            pltpu.VMEM((rows, width, width), BF),
            pltpu.VMEM((tags.shape[0], SLOTS * half + TAGS, wide), BF),
            pltpu.VMEM((5 * rows, half, wide), BF),
            pltpu.VMEM((4, width, width, rows), BF),
            pltpu.VMEM((group, width, wide), F32),
            pltpu.SemaphoreType.DMA((5,)),
            pltpu.SemaphoreType.DMA((rows // group,)),
            pltpu.SemaphoreType.DMA,
        ],
        compiler_params=params(),
        cost_estimate=pl.CostEstimate(
            flops=2 * rows * wide * wide * chunks * wide, bytes_accessed=30 * 2**20, transcendentals=0
        ),
        name="galerkin",
    )(index, position, tags, pltpu.with_memory_space_constraint(turned, pltpu.VMEM), own, *pieces)


def restore_kernel(ap_ref, out_ref):
    for g in range(0, ap_ref.shape[1], ROWS16):
        turned = jnp.swapaxes(ap_ref[:, g : g + ROWS16, :], 0, 1)
        for i in range(ROWS16):
            out_ref[g + i] = turned[i].T


def restore(ap):
    rows, width, _ = ap.shape
    return pl.pallas_call(
        restore_kernel,
        out_shape=jax.ShapeDtypeStruct((width, width, rows), BF),
        compiler_params=params(),
        cost_estimate=pl.CostEstimate(flops=0, bytes_accessed=8 * 2**20, transcendentals=0),
        name="restore",
    )(ap)


def sums_kernel(got_ref, out_ref):
    parts, height, wide = got_ref.shape
    half = wide // 4
    width = 2 * half
    tags = jnp.swapaxes(got_ref[:, SLOTS * half :, :], 0, 1)
    lane = lax.broadcasted_iota(jnp.int32, (parts, wide), 1) + 1
    chosen = [
        jnp.where(tags[s].astype(jnp.int32) == lane, 1.0, 0.0).T[:AGG_DEV].astype(BF)
        for s in range(SLOTS)
    ]
    chosen = jnp.concatenate(chosen, axis=1)
    for g in range(0, half, ROWS16):
        slots = [
            jnp.swapaxes(got_ref[:, s * half + g : s * half + g + ROWS16, :], 0, 1)
            for s in range(SLOTS)
        ]
        values = [
            jnp.dot(
                chosen,
                jnp.concatenate([slot[i] for slot in slots], axis=0),
                preferred_element_type=F32,
            )
            for i in range(ROWS16)
        ]
        value = jnp.swapaxes(jnp.stack(values), 0, 1)
        out_ref[:, g : g + ROWS16, :] = value[:, :, :width]
        out_ref[:, g + half : g + half + ROWS16, :] = value[:, :, width:]


def sums(got):
    parts, height, wide = got.shape
    width = wide // 2
    return pl.pallas_call(
        sums_kernel,
        in_specs=[WHOLE],
        out_specs=WHOLE,
        out_shape=jax.ShapeDtypeStruct((AGG_DEV, width, width), F32),
        compiler_params=params(),
        name="sums",
    )(got)


def shards(a_tiles, a_cols, p_tiles, aggregate):
    rows = p_tiles.shape[0]
    grid_x = lax.axis_size("px")
    grid_y = lax.axis_size("py")
    parts = grid_x * grid_y
    me_index = lax.axis_index("px") * grid_y + lax.axis_index("py")

    p_native = jnp.transpose(p_tiles, (1, 2, 0))
    own = own_tiles(p_native)
    pieces = []
    for axis in ("py", "px"):
        for step in (1, -1):
            pieces.append(passed_along(p_native, axis, step))

    cols = a_cols.T
    delta = cols // rows - me_index
    code = jnp.where(
        delta == 0,
        0,
        jnp.where(delta == -1, 1, jnp.where(delta == 1, 2, jnp.where(delta == -grid_y, 3, 4))),
    )
    index = code * rows + cols % rows

    owner = aggregate // AGG_DEV
    order = jnp.arange(rows, dtype=jnp.int32)
    earlier = (owner[:, None] == owner[None, :]) & (order[None, :] < order[:, None])
    rank = jnp.sum(earlier.astype(jnp.int32), axis=1)
    position = owner * SLOTS + rank
    spots = jnp.arange(parts * SLOTS, dtype=jnp.int32)
    placing = position[:, None] == spots[None, :]
    label = jnp.sum(jnp.where(placing, (aggregate % AGG_DEV + 1)[:, None], 0), axis=0)
    label = jnp.pad(label.astype(BF).reshape(parts, SLOTS), ((0, 0), (0, TAGS - SLOTS)))
    tags = jnp.broadcast_to(label[:, :, None], (parts, TAGS, 2 * p_tiles.shape[1]))

    a_native = jnp.transpose(a_tiles, (1, 2, 3, 0))
    a_native, index, position, tags, own = lax.optimization_barrier(
        (a_native, index, position, tags, own)
    )
    turned = turn_blocks(a_native)
    ap, send = galerkin(index, position, tags, turned, own, pieces)
    got = lax.all_to_all(send, BOTH, split_axis=0, concat_axis=0, tiled=True)
    ap_native = restore(ap)
    coarse = sums(got)
    return (jnp.transpose(ap_native, (2, 0, 1)), coarse)


def solution(mesh):
    return jax.shard_map(
        shards,
        mesh=mesh,
        in_specs=(
            P(BOTH, None, None, None),
            P(BOTH, None),
            P(BOTH, None, None),
            P(BOTH),
        ),
        out_specs=(P(BOTH, None, None), P(BOTH, None, None)),
        check_vma=False,
    )
```
